128 devices in a mesh: island: 4 (over y_hi, core), fsdp: 32 (over x, y_lo, z).
Axes of the slice: x: 4, y: 4 (y_hi: 2, y_lo: 2; y = y_hi * 2 + y_lo), z: 4, core: 2. Of those that a mesh axis runs over, the one named last changes fastest.
Arguments:
- tokens: bfloat16 [4, 16384, 8192], P('island', 'fsdp'), may hold values from -6 to 6
- cotangent: bfloat16 [4, 16384, 512], P('island', 'fsdp'), may hold values from -6 to 6
- weight: bfloat16 [4, 8192, 512], P('island', 'fsdp'), may hold values from -6 to 6
- moment_one: float32 [4, 8192, 512], P('island', 'fsdp'), may hold values from -4 to 4
- moment_two: float32 [4, 8192, 512], P('island', 'fsdp'), may hold values from 0.1 to 2
- step_count: int32 [4], P('island'), may hold values from 1 to 5, as said below
- outer_grad: float32 [4, 8192, 512], P('island', 'fsdp'), may hold values from -3 to 3
- outer_params: float32 [8192, 512], P('fsdp'), may hold values from -6 to 6
- outer_moment: float32 [8192, 512], P('fsdp'), may hold values from -3 to 3
Outputs:
- new_weight: bfloat16 [4, 8192, 512], P('island', 'fsdp')
- new_moment_one: float32 [4, 8192, 512], P('island', 'fsdp')
- new_moment_two: float32 [4, 8192, 512], P('island', 'fsdp')
- input_grad: bfloat16 [4, 16384, 8192], P('island', 'fsdp')
- new_outer_params: float32 [8192, 512], P('fsdp')
- new_outer_moment: float32 [8192, 512], P('fsdp')
The draws below stay inside these ranges and needn't reach their ends.
Inputs may be any that keep to these rules, and one draw needn't show every extreme that they name: `step_count`: some island's counter is 5 and another island's counter is 1; the others may take any value in the range, equal or not.
All inputs are finite; a program needn't handle non-finite values.
Results may differ from the reference program's by a relative error of at most 0.015.
Values may be sent and summed in bfloat16 or wider, within the bound.
No kernel may reach another device: no remote copies, remote signals or barrier semaphores. Data moves between devices by JAX's collectives and lax.ppermute only.
A program may use at most 192 MiB of HBM per device.

```python
import math
import jax
import jax.numpy as jnp
from jax import lax

D = 8192
KV = 512
TOK_DEV = 512
TOKENS = 16384
ISLANDS = 4
N_FSDP = 32


def draw_step_count(key, part):
    key = jax.random.fold_in(key, 17)
    key_pos, key_vals = jax.random.split(key)
    first = jax.random.randint(key_pos, (), 0, ISLANDS).astype(jnp.int32)
    values = jax.random.randint(key_vals, (ISLANDS,), 1, 6).astype(jnp.int32)
    places = jnp.arange(ISLANDS, dtype=jnp.int32)
    second = (first + 1) % ISLANDS
    values = jnp.where(places == first, 5, values)
    values = jnp.where(places == second, 1, values)
    return values.astype(jnp.int32)


def strengthened(result, own_key, source, target, shards_of, factor):
    owner, partner = [(jnp.arange(result.shape[axis_at]) // (result.shape[axis_at] // shards_of)).reshape([-1 if axis == axis_at else 1 for axis in range(result.ndim)]) for axis_at in (source, target)]
    chosen = jax.random.permutation(own_key, shards_of)[partner]
    strong = (owner == chosen) | (owner == (partner + shards_of // 2) % shards_of)
    return jnp.where(strong, factor * result, result)


def block_levels(own_key, extent, cuts, smallest, largest):
    gain, own = 1.0, jax.random.fold_in(own_key, 6)
    for dim, parts in cuts:
        heights = jnp.exp(jax.random.uniform(jax.random.fold_in(own, dim), (parts,), jnp.float32, smallest / len(cuts), largest / len(cuts)))
        gain = gain * jnp.repeat(heights, extent[dim] // parts).reshape([-1 if axis == dim else 1 for axis in range(len(extent))])
    return gain


def scatter_about(key, dims, deviation, limit, shards=(), kind=jnp.bfloat16):
    drawn = jax.random.normal(key, dims, jnp.float32) * deviation
    if len(shards) > 0:
        drawn = block_levels(key, dims, shards, -0.22, 0.18) * drawn
    return jnp.clip(drawn, min=-limit, max=limit).astype(kind)


def noise_with(key, extent, deviation, limit, cuts, heavy, kind=jnp.bfloat16):
    entries = deviation * jax.random.normal(key, extent, jnp.float32)
    if cuts:
        entries = entries * block_levels(key, extent, cuts, -0.22, 0.18)
    return jnp.clip(strengthened(entries, jax.random.fold_in(key, 3), *heavy), -limit, limit).astype(kind)


def setup_inputs(seed: int = 0) -> dict:
    streams_of = jax.random.split(jax.random.key(seed), 10)
    tokens = scatter_about(streams_of[0], (ISLANDS, TOKENS, D), 1.0, 6.0, ((0, 4), (1, 32)))
    cotangent = noise_with(streams_of[1], (ISLANDS, TOKENS, KV), 1.0, 6.0, ((0, 4), (1, 32)), (1, 2, 32, 2.75))
    weight = scatter_about(streams_of[2], (ISLANDS, D, KV), 1.0, 6.0, ((0, 4), (1, 32)))
    moment_one = scatter_about(streams_of[3], (ISLANDS, D, KV), 0.5, 4.0, ((0, 4), (1, 32)), jnp.float32)
    moment_two = jnp.clip(jnp.exp(math.log(2.0) - 2.9957323 * jax.random.uniform(streams_of[4], (ISLANDS, D, KV), jnp.float32) ** block_levels(streams_of[4], (ISLANDS, D, KV), ((0, 4), (1, 32)), -0.2, 0.2)), 0.1, 2.0)
    step_count = draw_step_count(jax.random.fold_in(streams_of[9], 71), 0)
    outer_grad = scatter_about(streams_of[6], (ISLANDS, D, KV), 0.3, 3.0, ((0, 4), (1, 32)), jnp.float32)
    outer_params = scatter_about(streams_of[7], (D, KV), 1.0, 6.0, ((0, 32),), jnp.float32)
    outer_moment = scatter_about(streams_of[8], (D, KV), 0.3, 3.0, ((0, 32),), jnp.float32)
    return {"tokens": tokens, "cotangent": cotangent, "weight": weight, "moment_one": moment_one, "moment_two": moment_two, "step_count": step_count, "outer_grad": outer_grad, "outer_params": outer_params, "outer_moment": outer_moment}


def island_step(tok, cot, wgt, mom_one, mom_two, t_float):
    scale = 1.0 / math.sqrt(D)
    xf = tok.astype(jnp.float32)
    inv_rms = lax.rsqrt(lax.optimization_barrier(jnp.mean(xf * xf, axis=-1, keepdims=True)) + 1e-05)
    normed = xf * inv_rms
    hidden = normed.astype(jnp.bfloat16)
    grad_h = (jnp.dot(cot, wgt.T, preferred_element_type=jnp.float32) * scale).astype(jnp.bfloat16)
    grad_hf = grad_h.astype(jnp.float32)
    input_grad = (inv_rms * (grad_hf - normed * lax.optimization_barrier(jnp.mean(grad_hf * normed, axis=-1, keepdims=True)))).astype(jnp.bfloat16)
    blocks_h = hidden.reshape(N_FSDP, TOK_DEV, D)
    blocks_c = cot.reshape(N_FSDP, TOK_DEV, KV)

    def add_block(total, pair):
        term = jnp.dot(pair[0].T, pair[1], preferred_element_type=jnp.float32) * scale
        return (total + term.astype(jnp.bfloat16).astype(jnp.float32), None)
    grad, unused = lax.scan(add_block, jnp.zeros((D, KV), jnp.float32), (blocks_h, blocks_c))
    new_one = 0.9 * mom_one + 0.1 * grad
    new_two = 0.95 * mom_two + 0.05 * grad * grad
    corr_one = 1.0 - jnp.power(jnp.float32(0.9), t_float)
    corr_two = 1.0 - jnp.power(jnp.float32(0.95), t_float)
    update = new_one / corr_one / (jnp.sqrt(new_two / corr_two) + 1e-08)
    wf = wgt.astype(jnp.float32)
    new_w = (wf - 0.15 * (update + 0.1 * wf)).astype(jnp.bfloat16)
    return (new_w, new_one, new_two, input_grad)

def reference(tokens, cotangent, weight, moment_one, moment_two, step_count, outer_grad, outer_params, outer_moment):
    weights_out, ones_out, twos_out, grads_out = ([], [], [], [])
    for isl in range(ISLANDS):
        t_float = step_count[isl].astype(jnp.float32)
        new_w, new_one, new_two, input_grad = island_step(tokens[isl], cotangent[isl], weight[isl], moment_one[isl], moment_two[isl], t_float)
        weights_out.append(new_w)
        ones_out.append(new_one)
        twos_out.append(new_two)
        grads_out.append(input_grad)
    delta = lax.optimization_barrier(jnp.sum(outer_grad, axis=0)) / ISLANDS
    new_outer_moment = 0.9 * outer_moment + delta
    new_outer_params = outer_params - 0.7 * (delta + 0.9 * new_outer_moment)
    return (jnp.stack(weights_out), jnp.stack(ones_out), jnp.stack(twos_out), jnp.stack(grads_out), new_outer_params, new_outer_moment)
```

```python
import functools
import math

import jax
import jax.numpy as jnp
from jax import lax
from jax.experimental import pallas as pl
from jax.experimental.pallas import tpu as pltpu
from jax.sharding import PartitionSpec as P

D = 8192
KV = 512
TOK = 512
NX, NY, NZ = 4, 2, 4
LANE = 128
HALF = 4 * LANE
SCALE = 1.0 / math.sqrt(D)
MIB = 1 << 20

HBM = pl.BlockSpec(memory_space=pl.ANY)
VMEM = pl.BlockSpec(memory_space=pltpu.VMEM)
SMEM = pl.BlockSpec(memory_space=pltpu.SMEM)


def in_hbm(a):
    return pltpu.with_memory_space_constraint(a, pltpu.HBM)


def place(x, y, z):
    return ((x % NX) * NY + y % NY) * NZ + z % NZ


def shift(a, dx, dy, dz):
    pairs = [
        (place(x, y, z), place(x + dx, y + dy, z + dz))
        for x in range(NX)
        for y in range(NY)
        for z in range(NZ)
    ]
    return lax.ppermute(a, "fsdp", pairs)


GROUP_A = [[place(x, y, z) for y in range(NY) for z in range(NZ)] for x in range(NX)]


def column(pos_ref, part, far, dy, near):
    x, y, z = pos_ref[0], pos_ref[1], pos_ref[2]
    if part == 0:
        block = (((x + far) & 3) * NY + dy) * NZ + near
    else:
        block = (((x + near) & 3) * NY + ((y + dy) & 1)) * NZ + ((z + far) & 3)
    return pl.ds(pl.multiple_of((block * 2 + part) * LANE, LANE), LANE)


CHUNK = 128


def stats_kernel(tok_ref, cot_ref, tokv_ref, inv_ref, cots_ref, sem):
    copies = [
        pltpu.make_async_copy(
            tok_ref.at[pl.ds(i * CHUNK, CHUNK)], tokv_ref.at[pl.ds(i * CHUNK, CHUNK)], sem.at[i]
        )
        for i in range(TOK // CHUNK)
    ]
    for c in copies:
        c.start()
    for i in range(TOK // CHUNK):
        copies[i].wait()

        def rows_of(r, carry, i=i):
            rows = pl.ds(pl.multiple_of(i * CHUNK + r * 64, 64), 64)
            acc = jnp.zeros((64, LANE), jnp.float32)
            for j in range(D // LANE):
                t = tokv_ref[rows, j * LANE : (j + 1) * LANE].astype(jnp.float32)
                acc = acc + t * t
            inv = lax.rsqrt(jnp.sum(acc, axis=-1, keepdims=True) * (1.0 / D) + 1e-05)
            inv_ref[rows, :] = jnp.broadcast_to(inv, (64, LANE))
            cots_ref[rows, :] = (cot_ref[rows, :].astype(jnp.float32) * (inv * SCALE)).astype(
                jnp.bfloat16
            )
            return carry

        lax.fori_loop(0, CHUNK // 64, rows_of, 0)


def stats(tok, cot):
    return pl.pallas_call(
        stats_kernel,
        in_specs=[pl.BlockSpec(memory_space=pltpu.HBM), VMEM],
        out_specs=[VMEM, VMEM, VMEM],
        out_shape=[
            pltpu.VMEM((TOK, D), jnp.bfloat16),
            jax.ShapeDtypeStruct((TOK, LANE), jnp.float32),
            jax.ShapeDtypeStruct((TOK, KV), jnp.bfloat16),
        ],
        scratch_shapes=[pltpu.SemaphoreType.DMA((TOK // CHUNK,))],
        compiler_params=pltpu.CompilerParams(vmem_limit_bytes=16 * MIB),
        cost_estimate=pl.CostEstimate(flops=3 * TOK * D, bytes_accessed=10 * MIB, transcendentals=TOK),
        name="token_stats",
    )(tok, cot)


def grad_kernel(parts, pos_ref, tokv_ref, cots_ref, *outs):
    cots = cots_ref[...]
    for (part, far, dy), out in zip(parts, outs, strict=True):
        a = jnp.concatenate(
            [tokv_ref[:, column(pos_ref, part, far, dy, near)] for near in range(4)], axis=1
        )
        out[...] = lax.dot_general(
            a, cots, (((0,), (0,)), ((), ())), preferred_element_type=jnp.float32
        ).astype(jnp.bfloat16)


def grad_terms(pos, tokv, cots, parts, name):
    n = len(parts)
    return pl.pallas_call(
        functools.partial(grad_kernel, parts),
        in_specs=[SMEM, VMEM, VMEM],
        out_specs=[VMEM] * n,
        out_shape=[jax.ShapeDtypeStruct((HALF, KV), jnp.bfloat16)] * n,
        compiler_params=pltpu.CompilerParams(vmem_limit_bytes=16 * MIB),
        cost_estimate=pl.CostEstimate(
            flops=2 * TOK * KV * HALF * n, bytes_accessed=MIB * n, transcendentals=0
        ),
        name=name,
    )(pos, tokv, cots)


def product(pos_ref, cot_ref, tokv_ref, w, which, store, total):
    prod = lax.dot_general(
        cot_ref[...], w, (((1,), (1,)), ((), ())), preferred_element_type=jnp.float32
    )
    for near in range(4):
        p = prod[:, near * LANE : (near + 1) * LANE]
        store(near, p.astype(jnp.bfloat16))
        total = total + p * tokv_ref[:, column(pos_ref, *which, near)].astype(jnp.float32)
    return total


def gradh_kernel(parts, n_pieces, pos_ref, cot_ref, tokv_ref, *rest):
    pieces = rest[:n_pieces]
    gh_ref, acc_ref, wbuf, sem = rest[n_pieces:]
    copies, at = [], 0
    for k, piece in enumerate(pieces):
        rows = piece.shape[0]
        copies.append(pltpu.make_async_copy(piece, wbuf.at[pl.ds(at, rows)], sem.at[k]))
        copies[-1].start()
        at += rows
    loaded = 0
    for i, which in enumerate(parts):
        while loaded < n_pieces and sum(p.shape[0] for p in pieces[:loaded]) <= i * HALF:
            copies[loaded].wait()
            loaded += 1

        def store(near, p, i=i):
            at = (i * 4 + near) * LANE
            gh_ref[:, at : at + LANE] = p

        total = jnp.zeros((TOK, LANE), jnp.float32) if i == 0 else acc_ref[...]
        w = wbuf[i * HALF : (i + 1) * HALF, :]
        acc_ref[...] = product(pos_ref, cot_ref, tokv_ref, w, which, store, total)


def gradh(pos, cot, tokv, parts, pieces, name):
    n = len(parts)
    return pl.pallas_call(
        functools.partial(gradh_kernel, parts, len(pieces)),
        in_specs=[SMEM, VMEM, VMEM] + [HBM] * len(pieces),
        out_specs=[VMEM, VMEM],
        out_shape=[
            jax.ShapeDtypeStruct((TOK, HALF * n), jnp.bfloat16),
            jax.ShapeDtypeStruct((TOK, LANE), jnp.float32),
        ],
        scratch_shapes=[
            pltpu.VMEM((HALF * n, KV), jnp.bfloat16),
            pltpu.SemaphoreType.DMA((len(pieces),)),
        ],
        compiler_params=pltpu.CompilerParams(vmem_limit_bytes=20 * MIB),
        cost_estimate=pl.CostEstimate(
            flops=2 * TOK * KV * HALF * n, bytes_accessed=MIB * n, transcendentals=0
        ),
        name=name,
    )(pos, cot, tokv, *[in_hbm(p) for p in pieces])


TILE = 64


def input_kernel(parts, last, n_acc, pos_ref, inv_ref, cot_ref, tokv_ref, *rest):
    accs, ghs = rest[:n_acc], rest[n_acc : 2 * n_acc]
    pieces = rest[2 * n_acc : 2 * n_acc + len(last)]
    out_ref, outv, ghv, acc, wbuf, sem_in, sem_out = rest[2 * n_acc + len(last) :]
    copies = [pltpu.make_async_copy(p, wbuf.at[k], sem_in.at[k]) for k, p in enumerate(pieces)]
    for copy in copies:
        copy.start()
    total = accs[0][...]
    for a in accs[1:]:
        total = total + a[...]
    acc[...] = total
    for i, which in enumerate(last):

        def store(near, p, i=i):
            at = (i * 4 + near) * LANE
            ghv[:, at : at + LANE] = p

        copies[i].wait()
        acc[...] = product(pos_ref, cot_ref, tokv_ref, wbuf[i], which, store, acc[...])
    sources = []
    for g, group in zip((*ghs, ghv), (*parts, last), strict=True):
        for i, which in enumerate(group):
            sources += [(g, i * 4 + near, (*which, near)) for near in range(4)]

    def copy_of(tile):
        slot = lax.rem(tile, 2)
        return pltpu.make_async_copy(
            outv.at[slot], out_ref.at[pl.ds(pl.multiple_of(tile * TILE, TILE), TILE)], sem_out.at[slot]
        )

    def emit(tile, carry):
        rows = pl.ds(pl.multiple_of(tile * TILE, TILE), TILE)
        slot = lax.rem(tile, 2)

        @pl.when(tile >= 2)
        def _():
            copy_of(tile - 2).wait()

        inv = inv_ref[rows, :]
        total = jnp.sum(acc[rows, :], axis=-1, keepdims=True)
        first = inv * SCALE
        second = inv * inv * inv * (total * (SCALE / D))
        for g, at, where in sources:
            col = column(pos_ref, *where)
            gh = g[rows, at * LANE : (at + 1) * LANE].astype(jnp.float32)
            t = tokv_ref[rows, col].astype(jnp.float32)
            outv[slot, :, col] = (first * gh - second * t).astype(jnp.bfloat16)
        copy_of(tile).start()
        return carry

    tiles = TOK // TILE
    lax.fori_loop(0, tiles, emit, 0)
    copy_of(jnp.int32(tiles - 2)).wait()
    copy_of(jnp.int32(tiles - 1)).wait()


def input_gradient(pos, inv, cot, tokv, accs, ghs, parts, last, pieces):
    return pl.pallas_call(
        functools.partial(input_kernel, parts, last, len(accs)),
        in_specs=[SMEM] + [VMEM] * (3 + 2 * len(accs)) + [HBM] * len(last),
        out_specs=HBM,
        out_shape=jax.ShapeDtypeStruct((TOK, D), jnp.bfloat16),
        scratch_shapes=[
            pltpu.VMEM((2, TILE, D), jnp.bfloat16),
            pltpu.VMEM((TOK, HALF * len(last)), jnp.bfloat16),
            pltpu.VMEM((TOK, LANE), jnp.float32),
            pltpu.VMEM((len(last), HALF, KV), jnp.bfloat16),
            pltpu.SemaphoreType.DMA((len(last),)),
            pltpu.SemaphoreType.DMA((2,)),
        ],
        compiler_params=pltpu.CompilerParams(vmem_limit_bytes=20 * MIB),
        cost_estimate=pl.CostEstimate(
            flops=TOK * KV * D, bytes_accessed=24 * MIB, transcendentals=0
        ),
        name="input_gradient",
    )(pos, inv, cot, tokv, *accs, *ghs, *[in_hbm(p) for p in pieces])


def sum_kernel(plan, n_in, *refs):
    outs = refs[n_in:]
    for k, runs in enumerate(plan):
        row = 0
        for rows, members in runs:
            total = None
            for ref, at in members:
                v = refs[ref][at : at + rows, :]
                v = v.astype(jnp.float32) if len(members) > 1 else v
                total = v if total is None else total + v
            outs[k][row : row + rows, :] = total.astype(jnp.bfloat16)
            row += rows


def sums(*outs):
    arrays, plan, sizes = [], [], []
    for runs in outs:
        plan.append([])
        for rows, members in runs:
            where = []
            for a, at in members:
                if not any(a is b for b in arrays):
                    arrays.append(a)
                where.append(([a is b for b in arrays].index(True), at))
            plan[-1].append((rows, where))
        sizes.append(sum(rows for rows, _ in runs))
    r = pl.pallas_call(
        functools.partial(sum_kernel, plan, len(arrays)),
        in_specs=[VMEM] * len(arrays),
        out_specs=[VMEM] * len(outs),
        out_shape=[jax.ShapeDtypeStruct((n, KV), jnp.bfloat16) for n in sizes],
        compiler_params=pltpu.CompilerParams(vmem_limit_bytes=8 * MIB),
        cost_estimate=pl.CostEstimate(
            flops=sum(sizes) * KV, bytes_accessed=MIB * len(arrays), transcendentals=0
        ),
        name="sum_terms",
    )(*arrays)
    return r[0] if len(outs) == 1 else r


def after(value, *others):
    return lax.optimization_barrier((value, *others))[0]


class Queue:
    def __init__(self, depth):
        self.depth, self.got = depth, []

    def turn(self, a):
        return after(a, self.got[-self.depth]) if len(self.got) >= self.depth else a

    def send(self, a, dx, dy, dz):
        self.got.append(shift(self.turn(a), dx, dy, dz))
        return self.got[-1]

    def swap(self, a, pairs):
        self.got.append(lax.ppermute(self.turn(a), "island", pairs))
        return self.got[-1]


def local(
    tokens,
    cotangent,
    weight,
    moment_one,
    moment_two,
    step_count,
    outer_grad,
    outer_params,
    outer_moment,
):
    tok, cot, wgt = tokens[0], cotangent[0], weight[0]
    f32, bf16 = jnp.float32, jnp.bfloat16
    me = lax.axis_index("fsdp")
    pos = jnp.stack([me // (NY * NZ), (me // NZ) % NY, me % NZ]).astype(jnp.int32)

    wa, wb = wgt[:LANE], wgt[LANE:]

    all_a = lax.all_gather(wa, "fsdp", axis=0, tiled=True, axis_index_groups=GROUP_A)
    nb1 = shift(wb, -1, 0, 0)
    nb3 = shift(wb, 1, 0, 0)
    nb2 = shift(wb, 2, 0, 0)

    near_b = sums([(LANE, [(w, 0)]) for w in (wb, nb1, nb2, nb3)])
    tokv, inv, cots = stats(tok, cot)
    cots = after(cots, near_b)
    ga20, ga21, gb20, gb21 = grad_terms(
        pos, tokv, cots, [(0, 2, 0), (0, 2, 1), (1, 2, 0), (1, 2, 1)], "grad_far"
    )

    def add(*xs):
        return sums([(xs[0].shape[0], [(x, 0) for x in xs])])

    q = Queue(5)
    ra_p = q.send(ga20, 1, 0, 0)
    ra_m = q.send(ga21, -1, 0, 0)
    rb_p = q.send(gb20, 0, 0, 1)
    rb_m = q.send(gb21, 0, 0, -1)
    yb = q.send(near_b, 0, 1, 0)
    ga11, ga30, gb11, gb30, ga10, ga31, gb10, gb31 = grad_terms(
        pos,
        tokv,
        cots,
        [(0, 1, 1), (0, 3, 0), (1, 1, 1), (1, 3, 0), (0, 1, 0), (0, 3, 1), (1, 1, 0), (1, 3, 1)],
        "grad_next",
    )
    pa1 = q.send(ga11, 1, 0, 0)
    ma0 = q.send(ga30, -1, 0, 0)
    pb1 = q.send(gb11, 0, 0, 1)
    mb0 = q.send(gb30, 0, 0, -1)
    mine = outer_grad[0].astype(bf16)
    swapped = q.swap(mine, [(0, 1), (1, 0), (2, 3), (3, 2)])
    pa0 = q.send(add(ga10, ra_p), 1, 0, 0)
    ma1 = q.send(add(ga31, ra_m), -1, 0, 0)
    pb0 = q.send(add(gb10, rb_p), 0, 0, 1)
    mb1 = q.send(add(gb31, rb_m), 0, 0, -1)
    pair = add(mine, swapped)
    other = q.swap(pair, [(0, 2), (2, 0), (1, 3), (3, 1)])
    ga00, ga01, gb00, gb01 = grad_terms(
        pos, tokv, cots, [(0, 0, 0), (0, 0, 1), (1, 0, 0), (1, 0, 1)], "grad_own"
    )
    a0, a1 = all_a[:HALF], all_a[HALF:]
    wa31 = q.send(a1, 1, 0, 0)
    wa10 = q.send(a0, -1, 0, 0)
    wb31 = q.send(yb, 0, 0, 1)
    wb10 = q.send(near_b, 0, 0, -1)
    own = [(0, 0, 0), (0, 0, 1), (1, 0, 0), (1, 0, 1)]
    gh1, acc1 = gradh(pos, cot, tokv, own, [all_a, near_b, yb], "gradh_own")
    sb = q.send(after(add(gb01, pb1, mb1), acc1), 0, 1, 0)
    wa30 = q.send(a0, 1, 0, 0)
    wa11 = q.send(a1, -1, 0, 0)
    wb30 = q.send(near_b, 0, 0, 1)
    wb11 = q.send(yb, 0, 0, -1)
    wa21 = q.send(wa31, 1, 0, 0)
    wa20 = q.send(wa10, -1, 0, 0)
    wb21 = q.send(wb31, 0, 0, 1)
    wb20 = q.send(wb10, 0, 0, -1)

    grad_a = lax.psum_scatter(
        sums([(HALF, [(a, 0) for a in (ga00, pa0, ma0)]), (HALF, [(a, 0) for a in (ga01, pa1, ma1)])]),
        "fsdp",
        scatter_dimension=0,
        tiled=True,
        axis_index_groups=GROUP_A,
    )
    t0, t1, t2, t3 = sums(*[[(LANE, [(a, k * LANE) for a in (gb00, pb0, mb0, sb)])] for k in range(4)])
    d1 = q.send(t1, 1, 0, 0)
    d3 = q.send(t3, -1, 0, 0)
    d2 = q.send(t2, 2, 0, 0)
    grad_b = (t0.astype(f32) + d1.astype(f32)) + (d2.astype(f32) + d3.astype(f32))
    grad = jnp.concatenate([grad_a.astype(f32), grad_b], axis=0)

    one = [(0, 3, 1), (0, 1, 0), (1, 3, 1), (1, 1, 0)]
    two = [(0, 3, 0), (0, 1, 1), (1, 3, 0), (1, 1, 1)]
    far = [(0, 2, 1), (0, 2, 0), (1, 2, 1), (1, 2, 0)]
    gh2, acc2 = gradh(pos, cot, tokv, one, [wa31, wa10, wb31, wb10], "gradh_one")
    gh3, acc3 = gradh(pos, cot, tokv, two, [wa30, wa11, wb30, wb11], "gradh_two")
    input_grad = input_gradient(
        pos,
        inv,
        cot,
        tokv,
        (acc1, acc2, acc3),
        (gh1, gh2, gh3),
        (own, one, two),
        far,
        (wa21, wa20, wb21, wb20),
    )

    t_float = step_count[0].astype(f32)
    new_one = 0.9 * moment_one[0] + 0.1 * grad
    new_two = 0.95 * moment_two[0] + 0.05 * grad * grad
    corr_one = 1.0 - jnp.power(jnp.float32(0.9), t_float)
    corr_two = 1.0 - jnp.power(jnp.float32(0.95), t_float)
    update = new_one / corr_one / (jnp.sqrt(new_two / corr_two) + 1e-08)
    wf = wgt.astype(f32)
    new_w = (wf - 0.15 * (update + 0.1 * wf)).astype(bf16)

    delta = (pair.astype(f32) + other.astype(f32)) / lax.axis_size("island")
    new_moment = 0.9 * outer_moment + delta
    new_params = outer_params - 0.7 * (delta + 0.9 * new_moment)
    return (new_w[None], new_one[None], new_two[None], input_grad[None], new_params, new_moment)


def solution(mesh):
    rows, mine = P("island", "fsdp", None), P("fsdp", None)
    return jax.shard_map(
        local,
        mesh=mesh,
        in_specs=(rows, rows, rows, rows, rows, P("island"), rows, mine, mine),
        out_specs=(rows, rows, rows, rows, mine, mine),
        check_vma=False,
    )
```

```python
import functools
import math

import jax
import jax.numpy as jnp
from jax import lax
from jax.experimental import pallas as pl
from jax.experimental.pallas import tpu as pltpu
from jax.sharding import PartitionSpec as P

D = 8192
KV = 512
TOK = 512
NX, NY, NZ = 4, 2, 4
LANE = 128
HALF = 4 * LANE
SCALE = 1.0 / math.sqrt(D)
MIB = 1 << 20

HBM = pl.BlockSpec(memory_space=pl.ANY)
VMEM = pl.BlockSpec(memory_space=pltpu.VMEM)
SMEM = pl.BlockSpec(memory_space=pltpu.SMEM)


def in_hbm(a):
    return pltpu.with_memory_space_constraint(a, pltpu.HBM)


def place(x, y, z):
    return ((x % NX) * NY + y % NY) * NZ + z % NZ


def shift(a, dx, dy, dz):
    pairs = [
        (place(x, y, z), place(x + dx, y + dy, z + dz))
        for x in range(NX)
        for y in range(NY)
        for z in range(NZ)
    ]
    return lax.ppermute(a, "fsdp", pairs)


GROUP_A = [[place(x, y, z) for y in range(NY) for z in range(NZ)] for x in range(NX)]


def column(pos_ref, part, far, dy, near):
    x, y, z = pos_ref[0], pos_ref[1], pos_ref[2]
    if part == 0:
        block = (((x + far) & 3) * NY + dy) * NZ + near
    else:
        block = (((x + near) & 3) * NY + ((y + dy) & 1)) * NZ + ((z + far) & 3)
    return pl.ds(pl.multiple_of((block * 2 + part) * LANE, LANE), LANE)


CHUNK = 128


def stats_kernel(tok_ref, cot_ref, tokv_ref, inv_ref, cots_ref, sem):
    copies = [
        pltpu.make_async_copy(
            tok_ref.at[pl.ds(i * CHUNK, CHUNK)], tokv_ref.at[pl.ds(i * CHUNK, CHUNK)], sem.at[i]
        )
        for i in range(TOK // CHUNK)
    ]
    for c in copies:
        c.start()
    for i in range(TOK // CHUNK):
        copies[i].wait()

        def rows_of(r, carry, i=i):
            rows = pl.ds(pl.multiple_of(i * CHUNK + r * 64, 64), 64)
            acc = jnp.zeros((64, LANE), jnp.float32)
            for j in range(D // LANE):
                t = tokv_ref[rows, j * LANE : (j + 1) * LANE].astype(jnp.float32)
                acc = acc + t * t
            inv = lax.rsqrt(jnp.sum(acc, axis=-1, keepdims=True) * (1.0 / D) + 1e-05)
            inv_ref[rows, :] = jnp.broadcast_to(inv, (64, LANE))
            cots_ref[rows, :] = (cot_ref[rows, :].astype(jnp.float32) * (inv * SCALE)).astype(
                jnp.bfloat16
            )
            return carry

        lax.fori_loop(0, CHUNK // 64, rows_of, 0)


def stats(tok, cot):
    return pl.pallas_call(
        stats_kernel,
        in_specs=[pl.BlockSpec(memory_space=pltpu.HBM), VMEM],
        out_specs=[VMEM, VMEM, VMEM],
        out_shape=[
            pltpu.VMEM((TOK, D), jnp.bfloat16),
            jax.ShapeDtypeStruct((TOK, LANE), jnp.float32),
            jax.ShapeDtypeStruct((TOK, KV), jnp.bfloat16),
        ],
        scratch_shapes=[pltpu.SemaphoreType.DMA((TOK // CHUNK,))],
        compiler_params=pltpu.CompilerParams(vmem_limit_bytes=16 * MIB),
        cost_estimate=pl.CostEstimate(flops=3 * TOK * D, bytes_accessed=10 * MIB, transcendentals=TOK),
        name="token_stats",
    )(tok, cot)


def grad_kernel(parts, pos_ref, tokv_ref, cots_ref, *outs):
    cots = cots_ref[...]
    for (part, far, dy), out in zip(parts, outs, strict=True):
        a = jnp.concatenate(
            [tokv_ref[:, column(pos_ref, part, far, dy, near)] for near in range(4)], axis=1
        )
        out[...] = lax.dot_general(
            a, cots, (((0,), (0,)), ((), ())), preferred_element_type=jnp.float32
        ).astype(jnp.bfloat16)


def grad_terms(pos, tokv, cots, parts, name):
    n = len(parts)
    return pl.pallas_call(
        functools.partial(grad_kernel, parts),
        in_specs=[SMEM, VMEM, VMEM],
        out_specs=[VMEM] * n,
        out_shape=[jax.ShapeDtypeStruct((HALF, KV), jnp.bfloat16)] * n,
        compiler_params=pltpu.CompilerParams(vmem_limit_bytes=16 * MIB),
        cost_estimate=pl.CostEstimate(
            flops=2 * TOK * KV * HALF * n, bytes_accessed=MIB * n, transcendentals=0
        ),
        name=name,
    )(pos, tokv, cots)


def product(pos_ref, cot_ref, tokv_ref, w, which, store, total):
    prod = lax.dot_general(
        cot_ref[...], w, (((1,), (1,)), ((), ())), preferred_element_type=jnp.float32
    )
    for near in range(4):
        p = prod[:, near * LANE : (near + 1) * LANE]
        store(near, p.astype(jnp.bfloat16))
        total = total + p * tokv_ref[:, column(pos_ref, *which, near)].astype(jnp.float32)
    return total


def gradh_kernel(parts, n_pieces, pos_ref, cot_ref, tokv_ref, *rest):
    pieces = rest[:n_pieces]
    gh_ref, acc_ref, wbuf, sem = rest[n_pieces:]
    copies, at = [], 0
    for k, piece in enumerate(pieces):
        rows = piece.shape[0]
        copies.append(pltpu.make_async_copy(piece, wbuf.at[pl.ds(at, rows)], sem.at[k]))
        copies[-1].start()
        at += rows
    loaded = 0
    for i, which in enumerate(parts):
        while loaded < n_pieces and sum(p.shape[0] for p in pieces[:loaded]) <= i * HALF:
            copies[loaded].wait()
            loaded += 1

        def store(near, p, i=i):
            at = (i * 4 + near) * LANE
            gh_ref[:, at : at + LANE] = p

        total = jnp.zeros((TOK, LANE), jnp.float32) if i == 0 else acc_ref[...]
        w = wbuf[i * HALF : (i + 1) * HALF, :]
        acc_ref[...] = product(pos_ref, cot_ref, tokv_ref, w, which, store, total)


def gradh(pos, cot, tokv, parts, pieces, name):
    n = len(parts)
    return pl.pallas_call(
        functools.partial(gradh_kernel, parts, len(pieces)),
        in_specs=[SMEM, VMEM, VMEM] + [HBM] * len(pieces),
        out_specs=[VMEM, VMEM],
        out_shape=[
            jax.ShapeDtypeStruct((TOK, HALF * n), jnp.bfloat16),
            jax.ShapeDtypeStruct((TOK, LANE), jnp.float32),
        ],
        scratch_shapes=[
            pltpu.VMEM((HALF * n, KV), jnp.bfloat16),
            pltpu.SemaphoreType.DMA((len(pieces),)),
        ],
        compiler_params=pltpu.CompilerParams(vmem_limit_bytes=20 * MIB),
        cost_estimate=pl.CostEstimate(
            flops=2 * TOK * KV * HALF * n, bytes_accessed=MIB * n, transcendentals=0
        ),
        name=name,
    )(pos, cot, tokv, *[in_hbm(p) for p in pieces])


TILE = 64


def input_kernel(parts, last, n_acc, pos_ref, inv_ref, cot_ref, tokv_ref, *rest):
    accs, ghs = rest[:n_acc], rest[n_acc : 2 * n_acc]
    pieces = rest[2 * n_acc : 2 * n_acc + len(last)]
    out_ref, outv, ghv, acc, sem_out = rest[2 * n_acc + len(last) :]
    total = accs[0][...]
    for a in accs[1:]:
        total = total + a[...]
    acc[...] = total
    for i, which in enumerate(last):

        def store(near, p, i=i):
            at = (i * 4 + near) * LANE
            ghv[:, at : at + LANE] = p

        acc[...] = product(pos_ref, cot_ref, tokv_ref, pieces[i][...], which, store, acc[...])
    sources = []
    for g, group in zip((*ghs, ghv), (*parts, last), strict=True):
        for i, which in enumerate(group):
            sources += [(g, i * 4 + near, (*which, near)) for near in range(4)]

    def copy_of(tile):
        slot = lax.rem(tile, 2)
        return pltpu.make_async_copy(
            outv.at[slot], out_ref.at[pl.ds(pl.multiple_of(tile * TILE, TILE), TILE)], sem_out.at[slot]
        )

    def emit(tile, carry):
        rows = pl.ds(pl.multiple_of(tile * TILE, TILE), TILE)
        slot = lax.rem(tile, 2)

        @pl.when(tile >= 2)
        def _():
            copy_of(tile - 2).wait()

        inv = inv_ref[rows, :]
        total = jnp.sum(acc[rows, :], axis=-1, keepdims=True)
        first = inv * SCALE
        second = inv * inv * inv * (total * (SCALE / D))
        for g, at, where in sources:
            col = column(pos_ref, *where)
            gh = g[rows, at * LANE : (at + 1) * LANE].astype(jnp.float32)
            t = tokv_ref[rows, col].astype(jnp.float32)
            outv[slot, :, col] = (first * gh - second * t).astype(jnp.bfloat16)
        copy_of(tile).start()
        return carry

    tiles = TOK // TILE
    lax.fori_loop(0, tiles, emit, 0)
    copy_of(jnp.int32(tiles - 2)).wait()
    copy_of(jnp.int32(tiles - 1)).wait()


def input_gradient(pos, inv, cot, tokv, accs, ghs, parts, last, pieces):
    return pl.pallas_call(
        functools.partial(input_kernel, parts, last, len(accs)),
        in_specs=[SMEM] + [VMEM] * (3 + 2 * len(accs) + len(last)),
        out_specs=HBM,
        out_shape=jax.ShapeDtypeStruct((TOK, D), jnp.bfloat16),
        scratch_shapes=[
            pltpu.VMEM((2, TILE, D), jnp.bfloat16),
            pltpu.VMEM((TOK, HALF * len(last)), jnp.bfloat16),
            pltpu.VMEM((TOK, LANE), jnp.float32),
            pltpu.SemaphoreType.DMA((2,)),
        ],
        compiler_params=pltpu.CompilerParams(vmem_limit_bytes=20 * MIB),
        cost_estimate=pl.CostEstimate(
            flops=TOK * KV * D, bytes_accessed=24 * MIB, transcendentals=0
        ),
        name="input_gradient",
    )(pos, inv, cot, tokv, *accs, *ghs, *pieces)


def sum_kernel(plan, n_in, *refs):
    outs = refs[n_in:]
    for k, runs in enumerate(plan):
        row = 0
        for rows, members in runs:
            total = None
            for ref, at in members:
                v = refs[ref][at : at + rows, :]
                v = v.astype(jnp.float32) if len(members) > 1 else v
                total = v if total is None else total + v
            outs[k][row : row + rows, :] = total.astype(jnp.bfloat16)
            row += rows


def sums(*outs):
    arrays, plan, sizes = [], [], []
    for runs in outs:
        plan.append([])
        for rows, members in runs:
            where = []
            for a, at in members:
                if not any(a is b for b in arrays):
                    arrays.append(a)
                where.append(([a is b for b in arrays].index(True), at))
            plan[-1].append((rows, where))
        sizes.append(sum(rows for rows, _ in runs))
    r = pl.pallas_call(
        functools.partial(sum_kernel, plan, len(arrays)),
        in_specs=[VMEM] * len(arrays),
        out_specs=[VMEM] * len(outs),
        out_shape=[jax.ShapeDtypeStruct((n, KV), jnp.bfloat16) for n in sizes],
        compiler_params=pltpu.CompilerParams(vmem_limit_bytes=8 * MIB),
        cost_estimate=pl.CostEstimate(
            flops=sum(sizes) * KV, bytes_accessed=MIB * len(arrays), transcendentals=0
        ),
        name="sum_terms",
    )(*arrays)
    return r[0] if len(outs) == 1 else r


def after(value, *others):
    return lax.optimization_barrier((value, *others))[0]


class Queue:
    def __init__(self, depth):
        self.depth, self.got = depth, []

    def turn(self, a):
        return after(a, self.got[-self.depth]) if len(self.got) >= self.depth else a

    def send(self, a, dx, dy, dz):
        self.got.append(shift(self.turn(a), dx, dy, dz))
        return self.got[-1]

    def swap(self, a, pairs):
        self.got.append(lax.ppermute(self.turn(a), "island", pairs))
        return self.got[-1]


def local(
    tokens,
    cotangent,
    weight,
    moment_one,
    moment_two,
    step_count,
    outer_grad,
    outer_params,
    outer_moment,
):
    tok, cot, wgt = tokens[0], cotangent[0], weight[0]
    f32, bf16 = jnp.float32, jnp.bfloat16
    me = lax.axis_index("fsdp")
    pos = jnp.stack([me // (NY * NZ), (me // NZ) % NY, me % NZ]).astype(jnp.int32)

    wa, wb = wgt[:LANE], wgt[LANE:]

    all_a = lax.all_gather(wa, "fsdp", axis=0, tiled=True, axis_index_groups=GROUP_A)
    nb1 = shift(wb, -1, 0, 0)
    nb3 = shift(wb, 1, 0, 0)
    nb2 = shift(wb, 2, 0, 0)

    near_b = sums([(LANE, [(w, 0)]) for w in (wb, nb1, nb2, nb3)])
    tokv, inv, cots = stats(tok, cot)
    cots = after(cots, near_b)
    ga20, ga21, gb20, gb21 = grad_terms(
        pos, tokv, cots, [(0, 2, 0), (0, 2, 1), (1, 2, 0), (1, 2, 1)], "grad_far"
    )

    def add(*xs):
        return sums([(xs[0].shape[0], [(x, 0) for x in xs])])

    q = Queue(5)
    ra_p = q.send(ga20, 1, 0, 0)
    ra_m = q.send(ga21, -1, 0, 0)
    rb_p = q.send(gb20, 0, 0, 1)
    rb_m = q.send(gb21, 0, 0, -1)
    yb = q.send(near_b, 0, 1, 0)
    ga11, ga30, gb11, gb30, ga10, ga31, gb10, gb31 = grad_terms(
        pos,
        tokv,
        cots,
        [(0, 1, 1), (0, 3, 0), (1, 1, 1), (1, 3, 0), (0, 1, 0), (0, 3, 1), (1, 1, 0), (1, 3, 1)],
        "grad_next",
    )
    pa1 = q.send(ga11, 1, 0, 0)
    ma0 = q.send(ga30, -1, 0, 0)
    pb1 = q.send(gb11, 0, 0, 1)
    mb0 = q.send(gb30, 0, 0, -1)
    own = [(0, 0, 0), (0, 0, 1), (1, 0, 0), (1, 0, 1)]
    gh1, acc1 = gradh(pos, cot, tokv, own, [all_a, near_b, yb], "gradh_own")
    mine = after(outer_grad[0].astype(bf16), acc1)
    swapped = q.swap(mine, [(0, 1), (1, 0), (2, 3), (3, 2)])
    pa0 = q.send(add(ga10, ra_p), 1, 0, 0)
    ma1 = q.send(add(ga31, ra_m), -1, 0, 0)
    pb0 = q.send(add(gb10, rb_p), 0, 0, 1)
    mb1 = q.send(add(gb31, rb_m), 0, 0, -1)
    pair = add(mine, swapped)
    other = q.swap(pair, [(0, 2), (2, 0), (1, 3), (3, 1)])
    ga00, ga01, gb00, gb01 = grad_terms(
        pos, tokv, cots, [(0, 0, 0), (0, 0, 1), (1, 0, 0), (1, 0, 1)], "grad_own"
    )
    a0, a1 = all_a[:HALF], all_a[HALF:]
    wa31 = q.send(a1, 1, 0, 0)
    wa10 = q.send(a0, -1, 0, 0)
    wb31 = q.send(yb, 0, 0, 1)
    wb10 = q.send(near_b, 0, 0, -1)
    sb = q.send(add(gb01, pb1, mb1), 0, 1, 0)
    wa30 = q.send(a0, 1, 0, 0)
    wa11 = q.send(a1, -1, 0, 0)
    wb30 = q.send(near_b, 0, 0, 1)
    wb11 = q.send(yb, 0, 0, -1)
    wa21 = q.send(wa31, 1, 0, 0)
    wa20 = q.send(wa10, -1, 0, 0)
    wb21 = q.send(wb31, 0, 0, 1)
    wb20 = q.send(wb10, 0, 0, -1)

    grad_a = lax.psum_scatter(
        sums([(HALF, [(a, 0) for a in (ga00, pa0, ma0)]), (HALF, [(a, 0) for a in (ga01, pa1, ma1)])]),
        "fsdp",
        scatter_dimension=0,
        tiled=True,
        axis_index_groups=GROUP_A,
    )
    t0, t1, t2, t3 = sums(*[[(LANE, [(a, k * LANE) for a in (gb00, pb0, mb0, sb)])] for k in range(4)])
    d1 = q.send(t1, 1, 0, 0)
    d3 = q.send(t3, -1, 0, 0)
    d2 = q.send(t2, 2, 0, 0)
    grad_b = (t0.astype(f32) + d1.astype(f32)) + (d2.astype(f32) + d3.astype(f32))
    grad = jnp.concatenate([grad_a.astype(f32), grad_b], axis=0)

    one = [(0, 3, 1), (0, 1, 0), (1, 3, 1), (1, 1, 0)]
    two = [(0, 3, 0), (0, 1, 1), (1, 3, 0), (1, 1, 1)]
    far = [(0, 2, 1), (0, 2, 0), (1, 2, 1), (1, 2, 0)]
    gh2, acc2 = gradh(pos, cot, tokv, one, [wa31, wa10, wb31, wb10], "gradh_one")
    gh3, acc3 = gradh(pos, cot, tokv, two, [wa30, wa11, wb30, wb11], "gradh_two")
    input_grad = input_gradient(
        pos,
        inv,
        cot,
        tokv,
        (acc1, acc2, acc3),
        (gh1, gh2, gh3),
        (own, one, two),
        far,
        (wa21, wa20, wb21, wb20),
    )

    t_float = step_count[0].astype(f32)
    new_one = 0.9 * moment_one[0] + 0.1 * grad
    new_two = 0.95 * moment_two[0] + 0.05 * grad * grad
    corr_one = 1.0 - jnp.power(jnp.float32(0.9), t_float)
    corr_two = 1.0 - jnp.power(jnp.float32(0.95), t_float)
    update = new_one / corr_one / (jnp.sqrt(new_two / corr_two) + 1e-08)
    wf = wgt.astype(f32)
    new_w = (wf - 0.15 * (update + 0.1 * wf)).astype(bf16)

    delta = (pair.astype(f32) + other.astype(f32)) / lax.axis_size("island")
    new_moment = 0.9 * outer_moment + delta
    new_params = outer_params - 0.7 * (delta + 0.9 * new_moment)
    return (new_w[None], new_one[None], new_two[None], input_grad[None], new_params, new_moment)


def solution(mesh):
    rows, mine = P("island", "fsdp", None), P("fsdp", None)
    return jax.shard_map(
        local,
        mesh=mesh,
        in_specs=(rows, rows, rows, rows, rows, P("island"), rows, mine, mine),
        out_specs=(rows, rows, rows, rows, mine, mine),
        check_vma=False,
    )
```

```python
import functools
import math

import jax
import jax.numpy as jnp
from jax import lax
from jax.experimental import pallas as pl
from jax.experimental.pallas import tpu as pltpu
from jax.sharding import PartitionSpec as P

D = 8192
KV = 512
TOK = 512
NX, NY, NZ = 4, 2, 4
LANE = 128
HALF = 4 * LANE
SCALE = 1.0 / math.sqrt(D)
MIB = 1 << 20

HBM = pl.BlockSpec(memory_space=pl.ANY)
VMEM = pl.BlockSpec(memory_space=pltpu.VMEM)
SMEM = pl.BlockSpec(memory_space=pltpu.SMEM)


def in_hbm(a):
    return pltpu.with_memory_space_constraint(a, pltpu.HBM)


def place(x, y, z):
    return ((x % NX) * NY + y % NY) * NZ + z % NZ


def shift(a, dx, dy, dz):
    pairs = [
        (place(x, y, z), place(x + dx, y + dy, z + dz))
        for x in range(NX)
        for y in range(NY)
        for z in range(NZ)
    ]
    return lax.ppermute(a, "fsdp", pairs)


GROUP_A = [[place(x, y, z) for y in range(NY) for z in range(NZ)] for x in range(NX)]


def column(pos_ref, part, far, dy, near):
    x, y, z = pos_ref[0], pos_ref[1], pos_ref[2]
    if part == 0:
        block = (((x + far) & 3) * NY + dy) * NZ + near
    else:
        block = (((x + near) & 3) * NY + ((y + dy) & 1)) * NZ + ((z + far) & 3)
    return pl.ds(pl.multiple_of((block * 2 + part) * LANE, LANE), LANE)


CHUNK = 128


def stats_kernel(tok_ref, cot_ref, tokv_ref, inv_ref, cots_ref, sem):
    copies = [
        pltpu.make_async_copy(
            tok_ref.at[pl.ds(i * CHUNK, CHUNK)], tokv_ref.at[pl.ds(i * CHUNK, CHUNK)], sem.at[i]
        )
        for i in range(TOK // CHUNK)
    ]
    for c in copies:
        c.start()
    for i in range(TOK // CHUNK):
        copies[i].wait()

        def rows_of(r, carry, i=i):
            rows = pl.ds(pl.multiple_of(i * CHUNK + r * 64, 64), 64)
            acc = jnp.zeros((64, LANE), jnp.float32)
            for j in range(D // LANE):
                t = tokv_ref[rows, j * LANE : (j + 1) * LANE].astype(jnp.float32)
                acc = acc + t * t
            inv = lax.rsqrt(jnp.sum(acc, axis=-1, keepdims=True) * (1.0 / D) + 1e-05)
            inv_ref[rows, :] = jnp.broadcast_to(inv, (64, LANE))
            cots_ref[rows, :] = (cot_ref[rows, :].astype(jnp.float32) * (inv * SCALE)).astype(
                jnp.bfloat16
            )
            return carry

        lax.fori_loop(0, CHUNK // 64, rows_of, 0)


def stats(tok, cot):
    return pl.pallas_call(
        stats_kernel,
        in_specs=[pl.BlockSpec(memory_space=pltpu.HBM), VMEM],
        out_specs=[VMEM, VMEM, VMEM],
        out_shape=[
            pltpu.VMEM((TOK, D), jnp.bfloat16),
            jax.ShapeDtypeStruct((TOK, LANE), jnp.float32),
            jax.ShapeDtypeStruct((TOK, KV), jnp.bfloat16),
        ],
        scratch_shapes=[pltpu.SemaphoreType.DMA((TOK // CHUNK,))],
        compiler_params=pltpu.CompilerParams(vmem_limit_bytes=16 * MIB),
        cost_estimate=pl.CostEstimate(flops=3 * TOK * D, bytes_accessed=10 * MIB, transcendentals=TOK),
        name="token_stats",
    )(tok, cot)


def grad_kernel(parts, pos_ref, tokv_ref, cots_ref, *outs):
    cots = cots_ref[...]
    for (part, far, dy), out in zip(parts, outs, strict=True):
        a = jnp.concatenate(
            [tokv_ref[:, column(pos_ref, part, far, dy, near)] for near in range(4)], axis=1
        )
        out[...] = lax.dot_general(
            a, cots, (((0,), (0,)), ((), ())), preferred_element_type=jnp.float32
        ).astype(jnp.bfloat16)


def grad_terms(pos, tokv, cots, parts, name):
    n = len(parts)
    return pl.pallas_call(
        functools.partial(grad_kernel, parts),
        in_specs=[SMEM, VMEM, VMEM],
        out_specs=[VMEM] * n,
        out_shape=[jax.ShapeDtypeStruct((HALF, KV), jnp.bfloat16)] * n,
        compiler_params=pltpu.CompilerParams(vmem_limit_bytes=16 * MIB),
        cost_estimate=pl.CostEstimate(
            flops=2 * TOK * KV * HALF * n, bytes_accessed=MIB * n, transcendentals=0
        ),
        name=name,
    )(pos, tokv, cots)


def product(pos_ref, cot_ref, tokv_ref, w, which, store, total):
    prod = lax.dot_general(
        cot_ref[...], w, (((1,), (1,)), ((), ())), preferred_element_type=jnp.float32
    )
    for near in range(4):
        p = prod[:, near * LANE : (near + 1) * LANE]
        store(near, p.astype(jnp.bfloat16))
        total = total + p * tokv_ref[:, column(pos_ref, *which, near)].astype(jnp.float32)
    return total


def gradh_kernel(parts, n_pieces, pos_ref, cot_ref, tokv_ref, *rest):
    pieces = rest[:n_pieces]
    gh_ref, acc_ref, wbuf, sem = rest[n_pieces:]
    copies, at = [], 0
    for k, piece in enumerate(pieces):
        rows = piece.shape[0]
        copies.append(pltpu.make_async_copy(piece, wbuf.at[pl.ds(at, rows)], sem.at[k]))
        copies[-1].start()
        at += rows
    loaded = 0
    for i, which in enumerate(parts):
        while loaded < n_pieces and sum(p.shape[0] for p in pieces[:loaded]) <= i * HALF:
            copies[loaded].wait()
            loaded += 1

        def store(near, p, i=i):
            at = (i * 4 + near) * LANE
            gh_ref[:, at : at + LANE] = p

        total = jnp.zeros((TOK, LANE), jnp.float32) if i == 0 else acc_ref[...]
        w = wbuf[i * HALF : (i + 1) * HALF, :]
        acc_ref[...] = product(pos_ref, cot_ref, tokv_ref, w, which, store, total)


def gradh(pos, cot, tokv, parts, pieces, name):
    n = len(parts)
    return pl.pallas_call(
        functools.partial(gradh_kernel, parts, len(pieces)),
        in_specs=[SMEM, VMEM, VMEM] + [HBM] * len(pieces),
        out_specs=[VMEM, VMEM],
        out_shape=[
            jax.ShapeDtypeStruct((TOK, HALF * n), jnp.bfloat16),
            jax.ShapeDtypeStruct((TOK, LANE), jnp.float32),
        ],
        scratch_shapes=[
            pltpu.VMEM((HALF * n, KV), jnp.bfloat16),
            pltpu.SemaphoreType.DMA((len(pieces),)),
        ],
        compiler_params=pltpu.CompilerParams(vmem_limit_bytes=20 * MIB),
        cost_estimate=pl.CostEstimate(
            flops=2 * TOK * KV * HALF * n, bytes_accessed=MIB * n, transcendentals=0
        ),
        name=name,
    )(pos, cot, tokv, *[in_hbm(p) for p in pieces])


TILE = 64


def input_kernel(parts, last, n_acc, pos_ref, inv_ref, cot_ref, tokv_ref, *rest):
    accs, ghs = rest[:n_acc], rest[n_acc : 2 * n_acc]
    pieces = rest[2 * n_acc : 2 * n_acc + len(last)]
    out_ref, outv, ghv, acc, sem_out = rest[2 * n_acc + len(last) :]
    total = accs[0][...]
    for a in accs[1:]:
        total = total + a[...]
    acc[...] = total
    for i, which in enumerate(last):

        def store(near, p, i=i):
            at = (i * 4 + near) * LANE
            ghv[:, at : at + LANE] = p

        acc[...] = product(pos_ref, cot_ref, tokv_ref, pieces[i][...], which, store, acc[...])
    sources = []
    for g, group in zip((*ghs, ghv), (*parts, last), strict=True):
        for i, which in enumerate(group):
            sources += [(g, i * 4 + near, (*which, near)) for near in range(4)]

    def copy_of(tile):
        slot = lax.rem(tile, 2)
        return pltpu.make_async_copy(
            outv.at[slot], out_ref.at[pl.ds(pl.multiple_of(tile * TILE, TILE), TILE)], sem_out.at[slot]
        )

    def emit(tile, carry):
        rows = pl.ds(pl.multiple_of(tile * TILE, TILE), TILE)
        slot = lax.rem(tile, 2)

        @pl.when(tile >= 2)
        def _():
            copy_of(tile - 2).wait()

        inv = inv_ref[rows, :]
        total = jnp.sum(acc[rows, :], axis=-1, keepdims=True)
        first = inv * SCALE
        second = inv * inv * inv * (total * (SCALE / D))
        for g, at, where in sources:
            col = column(pos_ref, *where)
            gh = g[rows, at * LANE : (at + 1) * LANE].astype(jnp.float32)
            t = tokv_ref[rows, col].astype(jnp.float32)
            outv[slot, :, col] = (first * gh - second * t).astype(jnp.bfloat16)
        copy_of(tile).start()
        return carry

    tiles = TOK // TILE
    lax.fori_loop(0, tiles, emit, 0)
    copy_of(jnp.int32(tiles - 2)).wait()
    copy_of(jnp.int32(tiles - 1)).wait()


def input_gradient(pos, inv, cot, tokv, accs, ghs, parts, last, pieces):
    return pl.pallas_call(
        functools.partial(input_kernel, parts, last, len(accs)),
        in_specs=[SMEM] + [VMEM] * (3 + 2 * len(accs) + len(last)),
        out_specs=HBM,
        out_shape=jax.ShapeDtypeStruct((TOK, D), jnp.bfloat16),
        scratch_shapes=[
            pltpu.VMEM((2, TILE, D), jnp.bfloat16),
            pltpu.VMEM((TOK, HALF * len(last)), jnp.bfloat16),
            pltpu.VMEM((TOK, LANE), jnp.float32),
            pltpu.SemaphoreType.DMA((2,)),
        ],
        compiler_params=pltpu.CompilerParams(vmem_limit_bytes=20 * MIB),
        cost_estimate=pl.CostEstimate(
            flops=TOK * KV * D, bytes_accessed=24 * MIB, transcendentals=0
        ),
        name="input_gradient",
    )(pos, inv, cot, tokv, *accs, *ghs, *pieces)


def sum_kernel(plan, n_in, *refs):
    outs = refs[n_in:]
    for k, runs in enumerate(plan):
        row = 0
        for rows, members in runs:
            total = None
            for ref, at in members:
                v = refs[ref][at : at + rows, :]
                v = v.astype(jnp.float32) if len(members) > 1 else v
                total = v if total is None else total + v
            outs[k][row : row + rows, :] = total.astype(jnp.bfloat16)
            row += rows


def sums(*outs):
    arrays, plan, sizes = [], [], []
    for runs in outs:
        plan.append([])
        for rows, members in runs:
            where = []
            for a, at in members:
                if not any(a is b for b in arrays):
                    arrays.append(a)
                where.append(([a is b for b in arrays].index(True), at))
            plan[-1].append((rows, where))
        sizes.append(sum(rows for rows, _ in runs))
    r = pl.pallas_call(
        functools.partial(sum_kernel, plan, len(arrays)),
        in_specs=[VMEM] * len(arrays),
        out_specs=[VMEM] * len(outs),
        out_shape=[jax.ShapeDtypeStruct((n, KV), jnp.bfloat16) for n in sizes],
        compiler_params=pltpu.CompilerParams(vmem_limit_bytes=8 * MIB),
        cost_estimate=pl.CostEstimate(
            flops=sum(sizes) * KV, bytes_accessed=MIB * len(arrays), transcendentals=0
        ),
        name="sum_terms",
    )(*arrays)
    return r[0] if len(outs) == 1 else r


def after(value, *others):
    return lax.optimization_barrier((value, *others))[0]


class Queue:
    def __init__(self, depth):
        self.depth, self.got = depth, []

    def turn(self, a):
        return after(a, self.got[-self.depth]) if len(self.got) >= self.depth else a

    def send(self, a, dx, dy, dz):
        self.got.append(shift(self.turn(a), dx, dy, dz))
        return self.got[-1]

    def swap(self, a, pairs):
        self.got.append(lax.ppermute(self.turn(a), "island", pairs))
        return self.got[-1]


def local(
    tokens,
    cotangent,
    weight,
    moment_one,
    moment_two,
    step_count,
    outer_grad,
    outer_params,
    outer_moment,
):
    tok, cot, wgt = tokens[0], cotangent[0], weight[0]
    f32, bf16 = jnp.float32, jnp.bfloat16
    me = lax.axis_index("fsdp")
    pos = jnp.stack([me // (NY * NZ), (me // NZ) % NY, me % NZ]).astype(jnp.int32)

    wa, wb = wgt[:LANE], wgt[LANE:]

    all_a = lax.all_gather(wa, "fsdp", axis=0, tiled=True, axis_index_groups=GROUP_A)
    nb1 = shift(wb, -1, 0, 0)
    nb3 = shift(wb, 1, 0, 0)
    nb2 = shift(wb, 2, 0, 0)

    near_b = sums([(LANE, [(w, 0)]) for w in (wb, nb1, nb2, nb3)])
    tokv, inv, cots = stats(tok, cot)
    cots = after(cots, near_b)
    ga20, ga21, gb20, gb21 = grad_terms(
        pos, tokv, cots, [(0, 2, 0), (0, 2, 1), (1, 2, 0), (1, 2, 1)], "grad_far"
    )

    def add(*xs):
        return sums([(xs[0].shape[0], [(x, 0) for x in xs])])

    q = Queue(5)
    ra_p = q.send(ga20, 1, 0, 0)
    ra_m = q.send(ga21, -1, 0, 0)
    rb_p = q.send(gb20, 0, 0, 1)
    rb_m = q.send(gb21, 0, 0, -1)
    yb = q.send(near_b, 0, 1, 0)
    ga11, ga30, gb11, gb30, ga10, ga31, gb10, gb31 = grad_terms(
        pos,
        tokv,
        cots,
        [(0, 1, 1), (0, 3, 0), (1, 1, 1), (1, 3, 0), (0, 1, 0), (0, 3, 1), (1, 1, 0), (1, 3, 1)],
        "grad_next",
    )
    pa1 = q.send(ga11, 1, 0, 0)
    ma0 = q.send(ga30, -1, 0, 0)
    pb1 = q.send(gb11, 0, 0, 1)
    mb0 = q.send(gb30, 0, 0, -1)
    mine = outer_grad[0].astype(bf16)
    swapped = q.swap(mine, [(0, 1), (1, 0), (2, 3), (3, 2)])
    pa0 = q.send(add(ga10, ra_p), 1, 0, 0)
    ma1 = q.send(add(ga31, ra_m), -1, 0, 0)
    pb0 = q.send(add(gb10, rb_p), 0, 0, 1)
    mb1 = q.send(add(gb31, rb_m), 0, 0, -1)
    pair = add(mine, swapped)
    own = [(0, 0, 0), (0, 0, 1), (1, 0, 0), (1, 0, 1)]
    gh1, acc1 = gradh(pos, cot, tokv, own, [all_a, near_b, yb], "gradh_own")
    other = q.swap(after(pair, acc1), [(0, 2), (2, 0), (1, 3), (3, 1)])
    ga00, ga01, gb00, gb01 = grad_terms(
        pos, tokv, cots, [(0, 0, 0), (0, 0, 1), (1, 0, 0), (1, 0, 1)], "grad_own"
    )
    a0, a1 = all_a[:HALF], all_a[HALF:]
    wa31 = q.send(a1, 1, 0, 0)
    wa10 = q.send(a0, -1, 0, 0)
    wb31 = q.send(yb, 0, 0, 1)
    wb10 = q.send(near_b, 0, 0, -1)
    sb = q.send(add(gb01, pb1, mb1), 0, 1, 0)
    wa30 = q.send(a0, 1, 0, 0)
    wa11 = q.send(a1, -1, 0, 0)
    wb30 = q.send(near_b, 0, 0, 1)
    wb11 = q.send(yb, 0, 0, -1)
    wa21 = q.send(wa31, 1, 0, 0)
    wa20 = q.send(wa10, -1, 0, 0)
    wb21 = q.send(wb31, 0, 0, 1)
    wb20 = q.send(wb10, 0, 0, -1)

    grad_a = lax.psum_scatter(
        sums([(HALF, [(a, 0) for a in (ga00, pa0, ma0)]), (HALF, [(a, 0) for a in (ga01, pa1, ma1)])]),
        "fsdp",
        scatter_dimension=0,
        tiled=True,
        axis_index_groups=GROUP_A,
    )
    t0, t1, t2, t3 = sums(*[[(LANE, [(a, k * LANE) for a in (gb00, pb0, mb0, sb)])] for k in range(4)])
    d1 = q.send(t1, 1, 0, 0)
    d3 = q.send(t3, -1, 0, 0)
    d2 = q.send(t2, 2, 0, 0)
    grad_b = (t0.astype(f32) + d1.astype(f32)) + (d2.astype(f32) + d3.astype(f32))
    grad = jnp.concatenate([grad_a.astype(f32), grad_b], axis=0)

    one = [(0, 3, 1), (0, 1, 0), (1, 3, 1), (1, 1, 0)]
    two = [(0, 3, 0), (0, 1, 1), (1, 3, 0), (1, 1, 1)]
    far = [(0, 2, 1), (0, 2, 0), (1, 2, 1), (1, 2, 0)]
    gh2, acc2 = gradh(pos, cot, tokv, one, [wa31, wa10, wb31, wb10], "gradh_one")
    gh3, acc3 = gradh(pos, cot, tokv, two, [wa30, wa11, wb30, wb11], "gradh_two")
    input_grad = input_gradient(
        pos,
        inv,
        cot,
        tokv,
        (acc1, acc2, acc3),
        (gh1, gh2, gh3),
        (own, one, two),
        far,
        (wa21, wa20, wb21, wb20),
    )

    t_float = step_count[0].astype(f32)
    new_one = 0.9 * moment_one[0] + 0.1 * grad
    new_two = 0.95 * moment_two[0] + 0.05 * grad * grad
    corr_one = 1.0 - jnp.power(jnp.float32(0.9), t_float)
    corr_two = 1.0 - jnp.power(jnp.float32(0.95), t_float)
    update = new_one / corr_one / (jnp.sqrt(new_two / corr_two) + 1e-08)
    wf = wgt.astype(f32)
    new_w = (wf - 0.15 * (update + 0.1 * wf)).astype(bf16)

    delta = (pair.astype(f32) + other.astype(f32)) / lax.axis_size("island")
    new_moment = 0.9 * outer_moment + delta
    new_params = outer_params - 0.7 * (delta + 0.9 * new_moment)
    return (new_w[None], new_one[None], new_two[None], input_grad[None], new_params, new_moment)


def solution(mesh):
    rows, mine = P("island", "fsdp", None), P("fsdp", None)
    return jax.shard_map(
        local,
        mesh=mesh,
        in_specs=(rows, rows, rows, rows, rows, P("island"), rows, mine, mine),
        out_specs=(rows, rows, rows, rows, mine, mine),
        check_vma=False,
    )
```
